128 devices in a mesh: dp: 32 (over y_lo, z, x), owner: 4 (over y_hi, core).
Axes of the slice: x: 4, y: 4 (y_hi: 2, y_lo: 2; y = y_hi * 2 + y_lo), z: 4, core: 2. Of those that a mesh axis runs over, the one named last changes fastest.
Arguments:
- tokens: bfloat16 [16384, 1536], P('dp', 'owner'), may hold values from -6 to 6
- routes: int32 [16384, 4], P('dp'), may hold values from 0 to 31, as said below
- route_weights: float32 [16384, 4], P('dp'), may hold values from 0.1 to 0.6
- w_in: bfloat16 [32, 1536, 2, 1536], P('dp', None, None, 'owner'), may hold values from -0.15625 to 0.15625
- w_out: bfloat16 [32, 1536, 1536], P('dp', 'owner'), may hold values from -0.15625 to 0.15625
- d_out: bfloat16 [16384, 1536], P('dp', 'owner'), may hold values from -6 to 6
Outputs:
- mixed: bfloat16 [16384, 1536], P('dp', 'owner')
- token_grad: bfloat16 [16384, 1536], P('dp', 'owner')
- grad_in: float32 [32, 1536, 2, 1536], P('dp', None, None, 'owner')
- grad_out: float32 [32, 1536, 1536], P('dp', 'owner')
The draws below stay inside these ranges and needn't reach their ends.
Inputs may be any that keep to these rules, and one draw needn't show every extreme that they name: `routes`: for row t the four numbers are distinct and each is (t // 512 + j) mod 32 for some j from -2 to 2.
All inputs are finite; a program needn't handle non-finite values.
Results may differ from the reference program's by a relative error of at most 0.0052.
Values may be sent and summed in bfloat16 or wider, within the bound.
No kernel may reach another device: no remote copies, remote signals or barrier semaphores. Data moves between devices by JAX's collectives and lax.ppermute only.
A program may use at most 192 MiB of HBM per device.

```python
import jax
import jax.numpy as jnp
from jax import lax

D = 1536
F = 1536
TOK_DEV = 512
EXPERTS = 32
TOKENS = 16384
N_DP = 32


def draw_routes(key, part):
    key = jax.random.fold_in(key, 11)
    key_drop, key_turn = jax.random.split(key)
    dropped = jax.random.randint(key_drop, (TOKENS, 1), 0, 5).astype(jnp.int32)
    slot_index = jnp.arange(4, dtype=jnp.int32)[None, :]
    kept_offsets = slot_index + (slot_index >= dropped).astype(jnp.int32)
    rotation = jax.random.randint(key_turn, (TOKENS, 1), 0, 4).astype(jnp.int32)
    position_order = (slot_index + rotation) % 4
    chosen = jnp.take_along_axis(kept_offsets, position_order, axis=1)
    home_block = (jnp.arange(TOKENS, dtype=jnp.int32) // TOK_DEV)[:, None]
    return ((home_block + chosen - 2) % EXPERTS).astype(jnp.int32)


def steps_of(key, shape, shards, smallest, high):
    gain, own = 1.0, jax.random.fold_in(key, 6)
    for position, blocks in shards:
        steps = jnp.exp(jax.random.uniform(jax.random.fold_in(own, position), (blocks,), jnp.float32, smallest / len(shards), high / len(shards)))
        gain = gain * jnp.repeat(steps, shape[position] // blocks).reshape([-1 if axis == position else 1 for axis in range(len(shape))])
    return gain


def gaussian(own_key, shape, scale, most, cuts=(), kind=jnp.bfloat16):
    entries = scale * jax.random.normal(own_key, shape, jnp.float32)
    if cuts:
        entries = entries * steps_of(own_key, shape, cuts, -0.22, 0.18)
    return jnp.clip(entries, -most, most).astype(kind)


def setup_inputs(seed: int = 0) -> dict:
    splits = jax.random.split(jax.random.key(seed), 7)
    tokens = gaussian(splits[0], (TOKENS, D), 1.0, 6.0, ((0, 32), (1, 4)))
    routes = draw_routes(jax.random.fold_in(splits[6], 71), 0)
    route_weights = jnp.clip(0.1 + 0.5 * jax.random.uniform(splits[2], (TOKENS, 4), jnp.float32) ** steps_of(splits[2], (TOKENS, 4), ((0, 32),), -0.2, 0.2), 0.1, 0.6)
    w_in = gaussian(splits[3], (EXPERTS, D, 2, F), D ** -0.5, 0.15625, ((0, 32), (3, 4)))
    w_out = gaussian(splits[4], (EXPERTS, F, D), F ** -0.5, 0.15625, ((0, 32), (1, 4)))
    d_out = gaussian(splits[5], (TOKENS, D), 1.0, 6.0, ((0, 32), (1, 4)))
    return dict(tokens=tokens, routes=routes, route_weights=route_weights, w_in=w_in, w_out=w_out, d_out=d_out)


def narrow_value(value):
    return lax.optimization_barrier(value.astype(jnp.bfloat16)).astype(jnp.float32)


def chain_total(parts):
    lower = narrow_value(parts[1] + narrow_value(parts[0]))
    upper = narrow_value(parts[3] + narrow_value(parts[4]))
    return parts[2] + lower + upper


def reference(tokens, routes, route_weights, w_in, w_out, d_out):
    model_width = tokens.shape[1]
    unit_count = w_out.shape[1]
    token_blocks = tokens.reshape(N_DP, TOK_DEV, model_width)
    grad_blocks = d_out.reshape(N_DP, TOK_DEV, model_width)
    route_blocks = routes.reshape(N_DP, TOK_DEV, 4)
    weight_blocks = route_weights.reshape(N_DP, TOK_DEV, 4)
    offsets = jnp.arange(5, dtype=jnp.int32) - 2
    within = jnp.arange(TOK_DEV, dtype=jnp.int32)

    def expert_step(carry, expert_id):
        mixed_total, grad_total = carry
        blocks = ((expert_id + offsets) % N_DP).astype(jnp.int32)
        rows_in = token_blocks[blocks].reshape(-1, model_width)
        grad_rows = grad_blocks[blocks].reshape(-1, model_width)
        route_rows = route_blocks[blocks].reshape(-1, 4)
        weight_rows = weight_blocks[blocks].reshape(-1, 4)
        route_share = jnp.sum(jnp.where(route_rows == expert_id, weight_rows, jnp.float32(0.0)), axis=1)
        weight_in = w_in[expert_id].reshape(model_width, 2 * unit_count)
        weight_out = w_out[expert_id]
        gate_up = jnp.dot(rows_in, weight_in, preferred_element_type=jnp.float32)
        gate_part = gate_up[:, :unit_count]
        up_part = gate_up[:, unit_count:]
        sigmoid_gate = jax.nn.sigmoid(1.702 * gate_part)
        hidden = (route_share[:, None] * (up_part + 1.0) * gate_part * sigmoid_gate).astype(jnp.bfloat16)
        mixed_rows = jnp.dot(hidden, weight_out, preferred_element_type=jnp.float32)
        hidden_grad = lax.dot_general(grad_rows, weight_out, (((1,), (1,)), ((), ())), preferred_element_type=jnp.float32)
        act_grad = route_share[:, None] * hidden_grad
        up_grad = act_grad * gate_part * sigmoid_gate
        gate_grad = act_grad * (up_part + 1.0) * (sigmoid_gate + 1.702 * gate_part * sigmoid_gate * (1.0 - sigmoid_gate))
        pair_grad = jnp.concatenate([gate_grad, up_grad], axis=1).astype(jnp.bfloat16)
        input_grad = lax.dot_general(pair_grad, weight_in, (((1,), (1,)), ((), ())), preferred_element_type=jnp.float32)
        row_index = (blocks[:, None] * TOK_DEV + within[None, :]).reshape(-1).astype(jnp.int32)
        mixed_total = mixed_total.at[row_index].add(mixed_rows)
        grad_total = grad_total.at[row_index].add(input_grad)
        rows_wide = rows_in.reshape(5, TOK_DEV, model_width).astype(jnp.float32)
        pair_wide = pair_grad.reshape(5, TOK_DEV, 2 * unit_count).astype(jnp.float32)
        hidden_wide = hidden.reshape(5, TOK_DEV, unit_count).astype(jnp.float32)
        cotan_wide = grad_rows.reshape(5, TOK_DEV, model_width).astype(jnp.float32)
        part_in = jnp.einsum("btd,btg->bdg", rows_wide, pair_wide)
        part_out = jnp.einsum("btf,btd->bfd", hidden_wide, cotan_wide)
        in_total = chain_total([part_in[j] for j in range(5)])
        out_total = chain_total([part_out[j] for j in range(5)])
        return (mixed_total, grad_total), (in_total.reshape(model_width, 2, unit_count), out_total)

    start = (jnp.zeros((TOKENS, model_width), jnp.float32), jnp.zeros((TOKENS, model_width), jnp.float32))
    (mixed_total, grad_total), (grad_in, grad_out) = lax.scan(expert_step, start, jnp.arange(EXPERTS, dtype=jnp.int32))
    return mixed_total.astype(jnp.bfloat16), grad_total.astype(jnp.bfloat16), grad_in, grad_out
```

```python
import functools

import jax
import jax.numpy as jnp
from jax import lax
from jax.experimental import pallas as pl
from jax.experimental.pallas import tpu as pltpu
from jax.sharding import PartitionSpec as P

F32 = jnp.float32
BF16 = jnp.bfloat16
SLOTS = 8
PLANE = 16
NT = (((1,), (1,)), ((), ()))
TN = (((0,), (0,)), ((), ()))


def dot(lhs, rhs, dims=(((1,), (0,)), ((), ()))):
    return lax.dot_general(lhs, rhs, dims, preferred_element_type=F32)


def core_swap(value):
    return lax.ppermute(value, "owner", [(0, 1), (1, 0), (2, 3), (3, 2)])


def pair_swap(value):
    return lax.ppermute(value, "owner", [(0, 2), (1, 3), (2, 0), (3, 1)])


def hop(value, by, cross):
    perm = []
    for e in range(32):
        to = (e + by) % 32
        flip = 2 if cross and to // PLANE != e // PLANE else 0
        for o in range(4):
            perm.append((e * 4 + o, to * 4 + (o ^ flip)))
    return lax.ppermute(value, ("dp", "owner"), perm)


def expert_kernel(slot, half, pa, pb, win0, win1, wout0, wout1, oa, ob, hid, pair):
    width = pb.shape[1] // 2
    units = wout0.shape[0]
    ra = pl.ds(pl.multiple_of(half[0] * width, width), width)
    rb = pl.ds(pl.multiple_of((1 - half[0]) * width, width), width)
    ta, da = pa[:, :width], pa[:, width : 2 * width]
    tb, db = pb[:, :width], pb[:, width:]
    extra = pa[:, 2 * width :].astype(F32)
    lane = lax.broadcasted_iota(jnp.int32, extra.shape, 1)
    mine = (lane == slot) | (lane == slot + SLOTS)
    share = jnp.sum(jnp.where(mine, extra, 0.0), axis=1, keepdims=True)
    hiddens, pairs = [], []
    for win, wout in ((win0, wout0), (win1, wout1)):
        gate_up = dot(ta, win[ra, :]) + dot(tb, win[rb, :])
        act = dot(da, wout[:, ra], NT) + dot(db, wout[:, rb], NT)
        gate, up = gate_up[:, :units], gate_up[:, units:] + 1.0
        sig = jax.nn.sigmoid(1.702 * gate)
        gs = gate * sig
        hiddens.append((share * up * gs).astype(BF16))
        act = share * act
        up_grad = act * gs
        gate_grad = act * up * (sig + 1.702 * gs * (1.0 - sig))
        pairs.append((gate_grad.astype(BF16), up_grad.astype(BF16)))
    for q in range(2):
        hid[:, q * units : (q + 1) * units] = hiddens[q]
        pair[:, 2 * q * units : (2 * q + 1) * units] = pairs[q][0]
        pair[:, (2 * q + 1) * units : (2 * q + 2) * units] = pairs[q][1]
    for out, rows in ((oa, ra), (ob, rb)):
        out[:, :width] = (
            dot(hiddens[0], wout0[:, rows]) + dot(hiddens[1], wout1[:, rows])
        ).astype(out.dtype)
        out[:, width:] = (
            dot(pair[:, : 2 * units], win0[rows, :], NT)
            + dot(pair[:, 2 * units :], win1[rows, :], NT)
        ).astype(out.dtype)


def expert(half, pa, pb, weights, slot, out_dtype):
    rows, width2 = pb.shape
    units = weights[2].shape[0]
    vm = pl.BlockSpec(memory_space=pltpu.VMEM)
    flops = 2 * rows * width2 * units * 2 * 6
    return pl.pallas_call(
        functools.partial(expert_kernel, slot),
        out_shape=(
            jax.ShapeDtypeStruct((rows, width2), out_dtype),
            jax.ShapeDtypeStruct((rows, width2), out_dtype),
            jax.ShapeDtypeStruct((rows, 2 * units), BF16),
            jax.ShapeDtypeStruct((rows, 4 * units), BF16),
        ),
        in_specs=[pl.BlockSpec(memory_space=pltpu.SMEM)] + [vm] * 6,
        out_specs=(vm,) * 4,
        compiler_params=pltpu.CompilerParams(vmem_limit_bytes=32 * 2**20),
        cost_estimate=pl.CostEstimate(
            flops=flops, bytes_accessed=12 * 2**20, transcendentals=rows * units * 2
        ),
    )(half, pa, pb, *weights)


def weight_kernel(quarter, count, half, *refs):
    pas, pbs = refs[:count], refs[count : 2 * count]
    hids, pairs = refs[2 * count : 3 * count], refs[3 * count : 4 * count]
    gin, gout = refs[4 * count :]
    width = pbs[0].shape[1] // 2
    units = hids[0].shape[1] // 2
    ra = pl.ds(pl.multiple_of(half[0] * width, width), width)
    rb = pl.ds(pl.multiple_of((1 - half[0]) * width, width), width)
    hq = slice(quarter * units, (quarter + 1) * units)
    pq = slice(2 * quarter * units, 2 * (quarter + 1) * units)
    for pieces, rows in ((pas, ra), (pbs, rb)):
        total = dot(pieces[0][:, :width], pairs[0][:, pq], TN)
        for j in range(1, count):
            total += dot(pieces[j][:, :width], pairs[j][:, pq], TN)
        gin[rows, :] = total.astype(gin.dtype)
        total = dot(hids[0][:, hq], pieces[0][:, width : 2 * width], TN)
        for j in range(1, count):
            total += dot(hids[j][:, hq], pieces[j][:, width : 2 * width], TN)
        gout[:, rows] = total.astype(gout.dtype)


def weight_grads(half, pas, pbs, hids, pairs, quarter, out_dtype):
    count = len(pas)
    rows, width2 = pbs[0].shape
    units = hids[0].shape[1] // 2
    vm = pl.BlockSpec(memory_space=pltpu.VMEM)
    return pl.pallas_call(
        functools.partial(weight_kernel, quarter, count),
        out_shape=(
            jax.ShapeDtypeStruct((width2, 2 * units), out_dtype),
            jax.ShapeDtypeStruct((units, width2), out_dtype),
        ),
        in_specs=[pl.BlockSpec(memory_space=pltpu.SMEM)] + [vm] * (4 * count),
        out_specs=(vm, vm),
        compiler_params=pltpu.CompilerParams(vmem_limit_bytes=48 * 2**20),
        cost_estimate=pl.CostEstimate(
            flops=2 * count * rows * width2 * units * 3,
            bytes_accessed=18 * 2**20,
            transcendentals=0,
        ),
    )(half, *pas, *pbs, *hids, *pairs)


def local(tokens, routes, route_weights, w_in, w_out, d_out):
    position = lax.axis_index("dp")
    owner = lax.axis_index("owner")
    core = owner % 2
    half = (owner // 2).reshape(1).astype(jnp.int32)
    rows = tokens.shape[0] // 2
    width = tokens.shape[1]
    units = w_out.shape[1]

    def ordered(mine, other, axis):
        return jnp.where(
            core == 0,
            jnp.concatenate([mine, other], axis),
            jnp.concatenate([other, mine], axis),
        )

    both = jnp.concatenate([tokens, d_out], axis=1)
    mine = lax.dynamic_slice_in_dim(both, core * rows, rows, 0)
    other = core_swap(lax.dynamic_slice_in_dim(both, (1 - core) * rows, rows, 0))
    a0 = jnp.concatenate(
        [ordered(mine[:, :width], other[:, :width], 1), ordered(mine[:, width:], other[:, width:], 1)],
        axis=1,
    )
    b0 = pair_swap(a0)
    my_routes = lax.dynamic_slice_in_dim(routes, core * rows, rows, 0)
    my_weights = lax.dynamic_slice_in_dim(route_weights, core * rows, rows, 0)
    ids = (position + jnp.arange(5, dtype=jnp.int32) - 2) % 32
    share = jnp.sum(
        jnp.where(my_routes[:, :, None] == ids[None, None, :], my_weights[:, :, None], 0.0), axis=1
    )
    high = lax.reduce_precision(share, 8, 7)
    low = share - high
    pad = ((0, 0), (0, SLOTS - 5))
    extra = jnp.concatenate([jnp.pad(high, pad), jnp.pad(low, pad)], axis=1)
    extra = jnp.pad(extra, ((0, 0), (0, 128 - 2 * SLOTS))).astype(BF16)
    a0 = jnp.concatenate([a0, extra], axis=1)

    win = w_in[0].reshape(4 * width, 2 * units)
    weights = (win, core_swap(win), w_out[0], core_swap(w_out[0]))

    def send(a, b, by):
        edge = (position % PLANE) == (PLANE - 1 if by > 0 else 0)
        return hop(a, by, False), hop(jnp.where(edge, a[:, : 4 * width], b), by, True)

    up1 = send(a0, b0, 1)
    down1 = send(a0, b0, -1)
    up2 = send(*up1, 1)
    down2 = send(*down1, -1)

    own = expert(half, a0, b0, weights, 2, F32)
    near_up = expert(half, *up1, weights, 3, F32)
    near_down = expert(half, *down1, weights, 1, F32)
    far_up = expert(half, *up2, weights, 4, BF16)
    far_down = expert(half, *down2, weights, 0, BF16)

    def back(ra, rb, by):
        edge = (position % PLANE) == (0 if by > 0 else PLANE - 1)
        rb = hop(rb, by, True).astype(F32)
        ra = hop(ra, by, False).astype(F32)
        return ra + jnp.where(edge, rb, 0.0), jnp.where(edge, 0.0, rb)

    def joined(result, arrived):
        return (result[0] + arrived[0]).astype(BF16), (result[1] + arrived[1]).astype(BF16)

    from_up = back(*joined(near_up, back(far_up[0], far_up[1], -1)), -1)
    from_down = back(*joined(near_down, back(far_down[0], far_down[1], 1)), 1)
    total_b = (own[1] + from_up[1] + from_down[1]).astype(BF16)
    total = (own[0] + from_up[0] + from_down[0] + pair_swap(total_b).astype(F32)).astype(BF16)

    def quarter(index):
        at = index * width
        return jnp.concatenate(
            [
                lax.dynamic_slice_in_dim(total, at, width, 1),
                lax.dynamic_slice_in_dim(total, 2 * width + at, width, 1),
            ],
            axis=1,
        )

    result = ordered(quarter(core), core_swap(quarter(1 - core)), 0)
    mixed, token_grad = result[:, :width], result[:, width:]

    blocks = ((a0, b0), up1, down1, up2, down2)
    results = (own, near_up, near_down, far_up, far_down)
    pas, pbs = [p[0] for p in blocks], [p[1] for p in blocks]
    hids, pairs = [r[2] for r in results], [r[3] for r in results]
    gin_sent, gout_sent = weight_grads(half, pas, pbs, hids, pairs, 1, BF16)
    gin_got, gout_got = core_swap(gin_sent), core_swap(gout_sent)
    gin, gout = weight_grads(half, pas, pbs, hids, pairs, 0, F32)
    grad_in = (gin + gin_got.astype(F32)).reshape(1, 4 * width, 2, units)
    grad_out = (gout + gout_got.astype(F32))[None]
    return (mixed, token_grad, grad_in, grad_out)


def solution(mesh):
    placed = (
        P("dp", "owner"),
        P("dp", None),
        P("dp", None),
        P("dp", None, None, "owner"),
        P("dp", "owner", None),
        P("dp", "owner"),
    )
    return jax.shard_map(
        local,
        mesh=mesh,
        in_specs=placed,
        out_specs=(
            P("dp", "owner"),
            P("dp", "owner"),
            P("dp", None, None, "owner"),
            P("dp", "owner", None),
        ),
        check_vma=False,
    )
```

```python
import functools

import jax
import jax.numpy as jnp
from jax import lax
from jax.experimental import pallas as pl
from jax.experimental.pallas import tpu as pltpu
from jax.sharding import PartitionSpec as P

F32 = jnp.float32
BF16 = jnp.bfloat16
SLOTS = 8
PLANE = 16
NT = (((1,), (1,)), ((), ()))
TN = (((0,), (0,)), ((), ()))


def dot(lhs, rhs, dims=(((1,), (0,)), ((), ()))):
    return lax.dot_general(lhs, rhs, dims, preferred_element_type=F32)


def core_swap(value):
    return lax.ppermute(value, "owner", [(0, 1), (1, 0), (2, 3), (3, 2)])


def pair_swap(value):
    return lax.ppermute(value, "owner", [(0, 2), (1, 3), (2, 0), (3, 1)])


def hop(value, by, cross=False):
    perm = []
    for e in range(32):
        to = (e + by) % 32
        flip = 2 if cross and to // PLANE != e // PLANE else 0
        for o in range(4):
            perm.append((e * 4 + o, to * 4 + (o ^ flip)))
    return lax.ppermute(value, ("dp", "owner"), perm)


ANY = pl.BlockSpec(memory_space=pl.ANY)
HBM = pl.BlockSpec(memory_space=pltpu.HBM)
VMEM = pl.BlockSpec(memory_space=pltpu.VMEM)
SMEM = pl.BlockSpec(memory_space=pltpu.SMEM)
EXPERT_VMEM = 28 * 2**20
OTHER_VMEM = 60 * 2**20
SMALL_VMEM = 12 * 2**20


class Copies:
    def __init__(self, sems):
        self.sems, self.used = sems, 0

    def start(self, *pairs):
        copies = []
        for src, dst in pairs:
            copies.append(pltpu.make_async_copy(src, dst, self.sems.at[self.used]))
            self.used += 1
        for copy in copies:
            copy.start()
        return copies


def wait(copies):
    for copy in copies:
        copy.wait()


def pick_kernel(where, tokens, d_out, mine, rest, sems):
    rows, width = mine.shape[0], tokens.shape[1]
    copies, pairs = Copies(sems), []
    for core, out in ((where[1], mine), (1 - where[1], rest)):
        at = pl.ds(pl.multiple_of(core * rows, rows), rows)
        pairs.append((tokens.at[at, :], out.at[:, pl.ds(0, width)]))
        pairs.append((d_out.at[at, :], out.at[:, pl.ds(width, width)]))
    wait(copies.start(*pairs))


def join_kernel(where, mine, other, far_mine, far_other, extra, whole_t, whole_d, sems):
    width = mine.shape[1] // 2
    half, core = where[0], where[1]
    copies, pairs = Copies(sems), []
    for piece, h, c in (
        (mine, half, core),
        (other, half, 1 - core),
        (far_mine, 1 - half, core),
        (far_other, 1 - half, 1 - core),
    ):
        at = pl.ds(pl.multiple_of((h * 2 + c) * width, width), width)
        pairs.append((piece.at[:, pl.ds(0, width)], whole_t.at[:, at]))
        pairs.append((piece.at[:, pl.ds(width, width)], whole_d.at[:, at]))
    pairs.append((extra, whole_t.at[:, pl.ds(4 * width, extra.shape[1])]))
    wait(copies.start(*pairs))


def small_call(kernel, where, *operands, shapes):
    return pl.pallas_call(
        kernel,
        out_shape=tuple(jax.ShapeDtypeStruct(shape, BF16) for shape in shapes),
        in_specs=[SMEM] + [ANY] * len(operands),
        out_specs=(VMEM,) * len(shapes),
        scratch_shapes=[pltpu.SemaphoreType.DMA((9,))],
        compiler_params=pltpu.CompilerParams(vmem_limit_bytes=SMALL_VMEM),
        cost_estimate=pl.CostEstimate(flops=0, bytes_accessed=2 * 2**20, transcendentals=0),
    )(where, *operands)


def expert_kernel(phase, slots, n_in, where, *refs):
    ins, rest = refs[:n_in], list(refs[n_in:])
    with_t, with_d = phase != "d", phase != "t"
    count = len(slots)
    per = with_t + with_d
    sides = [ins[2 + per * i : 2 + per * (i + 1)] for i in range(count)]
    wide = 2 * ins[0].shape[1]
    units = (ins[0].shape[0] - wide) // 2
    halves = (slice(0, wide // 2), slice(wide // 2, wide))
    win = [w[:wide, :] for w in ins[:2]]
    wout = [[w[wide + k * units : wide + (k + 1) * units, :] for k in range(2)] for w in ins[:2]]
    rows = sides[0][0].shape[0]
    spans = [pl.ds(i * rows, rows) for i in range(count)]

    def take(n):
        return [rest.pop(0) for _ in range(n)]

    if with_t:
        mixed_outs, hid_outs = take(count), take(count)
    if phase == "t":
        fa_out, fb_out = take(2)
    if with_d:
        grad_outs, pair_outs = take(count), take(count)
    sems = rest.pop(-1)
    copies = Copies(sems)
    fa, fb = take(2)
    load_t, load_d, stores = [], [], []
    if with_t:
        xt, mixed, hid = take(3)
        for side, span in zip(sides, spans):
            load_t += copies.start((side[0], xt.at[span, :]))
    if with_d:
        xd, grad, pair = take(3)
        for side, span in zip(sides, spans):
            load_d += copies.start((side[-1], xd.at[span, :]))
    if not with_t:
        load_d += copies.start((ins[2 + per * count], fa), (ins[3 + per * count], fb))
    if with_t:
        wait(load_t)
        extra = xt[:, wide:].astype(F32)
        lane = lax.broadcasted_iota(jnp.int32, extra.shape, 1)
        row = lax.broadcasted_iota(jnp.int32, extra.shape, 0)
        slot = slots[0] if count == 1 else jnp.where(row < rows, slots[0], slots[1])
        mine = (lane == slot) | (lane == slot + SLOTS)
        share = jnp.sum(jnp.where(mine, extra, 0.0), axis=1, keepdims=True)
        for q in range(2):
            cols = slice(q * units, (q + 1) * units)
            gate_up = dot(xt[:, :wide], win[q])
            gate, up = gate_up[:, :units], gate_up[:, units:] + 1.0
            sig = jax.nn.sigmoid(1.702 * gate)
            gs = gate * sig
            sup = share * up
            hid[:, cols] = (sup * gs).astype(BF16)
            fa[:, cols] = sup * (sig + 1.702 * gs * (1.0 - sig))
            fb[:, cols] = share * gs
        for out, span in zip(hid_outs, spans):
            stores += copies.start((hid.at[span, :], out))
        if phase == "t":
            stores += copies.start((fa, fa_out), (fb, fb_out))
        for k, cols in enumerate(halves):
            total = dot(hid[:, :units], wout[0][k]) + dot(hid[:, units:], wout[1][k])
            mixed[:, cols] = total.astype(mixed.dtype)
        for out, span in zip(mixed_outs, spans):
            stores += copies.start((mixed.at[span, :], out))
    if with_d:
        wait(load_d)
        for q in range(2):
            cols = slice(q * units, (q + 1) * units)
            act = dot(xd[:, halves[0]], wout[q][0], NT) + dot(xd[:, halves[1]], wout[q][1], NT)
            pair[:, 2 * q * units : (2 * q + 1) * units] = (act * fa[:, cols]).astype(BF16)
            pair[:, (2 * q + 1) * units : (2 * q + 2) * units] = (act * fb[:, cols]).astype(BF16)
        for out, span in zip(pair_outs, spans):
            stores += copies.start((pair.at[span, :], out))
        grad[...] = (
            dot(pair[:, : 2 * units], win[0], NT) + dot(pair[:, 2 * units :], win[1], NT)
        ).astype(grad.dtype)
        for out, span in zip(grad_outs, spans):
            stores += copies.start((grad.at[span, :], out))
    wait(stores)


def expert(phase, where, weights, sides, slots, out_dtype, after=()):
    count = len(slots)
    rows = sides[0][0].shape[0]
    deep = count * rows
    wide = 2 * weights[0].shape[1]
    units = (weights[0].shape[0] - wide) // 2
    with_t, with_d = phase != "d", phase != "t"
    outs = []
    if with_t:
        outs += [((rows, wide), out_dtype)] * count + [((rows, 2 * units), BF16)] * count
    if phase == "t":
        outs += [((deep, 2 * units), F32)] * 2
    if with_d:
        outs += [((rows, wide), out_dtype)] * count + [((rows, 4 * units), BF16)] * count
    scratch = [((deep, 2 * units), F32)] * 2
    if with_t:
        scratch += [((deep, sides[0][0].shape[1]), BF16), ((deep, wide), out_dtype), ((deep, 2 * units), BF16)]
    if with_d:
        scratch += [((deep, wide), BF16), ((deep, wide), out_dtype), ((deep, 4 * units), BF16)]
    operands = (*weights, *[piece for side in sides for piece in side], *after)
    results = pl.pallas_call(
        functools.partial(expert_kernel, phase, slots, len(operands)),
        out_shape=tuple(jax.ShapeDtypeStruct(*o) for o in outs),
        in_specs=[SMEM] + [VMEM] * 2 + [HBM] * (len(operands) - 2),
        out_specs=(HBM,) * len(outs),
        scratch_shapes=[pltpu.VMEM(*v) for v in scratch] + [pltpu.SemaphoreType.DMA((16,))],
        compiler_params=pltpu.CompilerParams(vmem_limit_bytes=EXPERT_VMEM),
        cost_estimate=pl.CostEstimate(
            flops=2 * deep * wide * units * 2 * 3 * (with_t + with_d),
            bytes_accessed=12 * 2**20,
            transcendentals=deep * units * 2,
        ),
    )(where, *operands)
    results, named = list(results), {}
    for name, there, n in (
        ("m", with_t, count),
        ("hid", with_t, count),
        ("f", phase == "t", 2),
        ("g", with_d, count),
        ("pair", with_d, count),
    ):
        if there:
            named[name] = [results.pop(0) for _ in range(n)]
    return named


def weight_kernel(quarter, count, n_in, *refs):
    blocks = [refs[4 * j : 4 * j + 4] for j in range(count)]
    out, xt, xd, hid, pair, grads, sems = refs[n_in:]
    rows, wide = pair.shape[0] // count, xt.shape[1]
    units = hid.shape[1]
    copies = Copies(sems)
    first, second = [], []
    for j, (t, d, hids, pairs) in enumerate(blocks):
        block = pl.ds(j * rows, rows)
        first.append((pairs.at[:, pl.ds(2 * quarter * units, 2 * units)], pair.at[block, :]))
        first.append((t.at[:, pl.ds(0, wide)], xt.at[block, :]))
        second.append((hids.at[:, pl.ds(quarter * units, units)], hid.at[block, :]))
        second.append((d, xd.at[block, :]))
    first, second = copies.start(*first), copies.start(*second)
    wait(first)
    stores = []
    step = 256
    def keep(at, value):
        grads[at, :] = value.astype(grads.dtype)
        stores.extend(copies.start((grads.at[at, :], out.at[at, :])))

    for r in range(0, wide, step):
        keep(pl.ds(r, step), dot(xt[:, r : r + step], pair[...], TN))
    wait(second)
    for k in range(2):
        band = slice(k * wide // 2, (k + 1) * wide // 2)
        keep(pl.ds(wide + k * units, units), dot(hid[...], xd[:, band], TN))
    wait(stores)


def weight_grads(blocks, quarter, out_dtype, after=()):
    count = len(blocks)
    rows, wide = blocks[0][1].shape
    units = blocks[0][2].shape[1] // 2
    operands = [ref for block in blocks for ref in block] + list(after)
    depth = count * rows
    return pl.pallas_call(
        functools.partial(weight_kernel, quarter, count, len(operands)),
        out_shape=jax.ShapeDtypeStruct((wide + 2 * units, 2 * units), out_dtype),
        in_specs=[HBM] * len(operands),
        out_specs=HBM,
        scratch_shapes=[pltpu.VMEM((depth, n), BF16) for n in (wide, wide, units, 2 * units)]
        + [
            pltpu.VMEM((wide + 2 * units, 2 * units), out_dtype),
            pltpu.SemaphoreType.DMA((4 * count + 8,)),
        ],
        compiler_params=pltpu.CompilerParams(vmem_limit_bytes=OTHER_VMEM),
        cost_estimate=pl.CostEstimate(
            flops=2 * depth * wide * units * 3, bytes_accessed=18 * 2**20, transcendentals=0
        ),
    )(*operands)


def tied(values, *others):
    return lax.optimization_barrier((values, others))[0]


def local(tokens, routes, route_weights, w_in, w_out, d_out):
    position = lax.axis_index("dp")
    owner = lax.axis_index("owner")
    core = owner % 2
    where = jnp.stack([owner // 2, core]).astype(jnp.int32)
    rows = tokens.shape[0] // 2
    width = tokens.shape[1]
    units = w_out.shape[1]

    def part(value, index):
        return lax.dynamic_slice_in_dim(value, index * rows, rows, 0)

    ids = (position + jnp.arange(5, dtype=jnp.int32) - 2) % 32
    chosen = part(routes, core)[:, :, None] == ids[None, None, :]
    share = jnp.sum(jnp.where(chosen, part(route_weights, core)[:, :, None], 0.0), axis=1)
    high = lax.reduce_precision(share, 8, 7)
    low = share - high
    pad = ((0, 0), (0, SLOTS - 5))
    extra = jnp.concatenate([jnp.pad(high, pad), jnp.pad(low, pad)], axis=1)
    extra = jnp.pad(extra, ((0, 0), (0, 128 - 2 * SLOTS))).astype(BF16)
    mine, rest = small_call(pick_kernel, where, tokens, d_out, shapes=[(rows, 2 * width)] * 2)
    far_mine = pair_swap(mine)
    other = core_swap(rest)
    far_other = pair_swap(other)
    t0, d0 = small_call(
        join_kernel, where, mine, other, far_mine, far_other, extra,
        shapes=[(rows, 4 * width + 128), (rows, 4 * width)],
    )

    w_in, w_out = tied((w_in[0], w_out[0]), t0)
    packed = jnp.concatenate(
        [w_in.reshape(4 * width, 2 * units), w_out[:, : 2 * width], w_out[:, 2 * width :]], axis=0
    )
    weights = (packed, core_swap(packed))

    up1t, down1t = hop(t0, 1), hop(t0, -1)
    up1d, down1d = hop(d0, 1, True), hop(d0, -1, True)
    up2t, down2t = hop(up1t, 1), hop(down1t, -1)
    own = expert("td", where, weights, [(t0, d0)], (2,), F32)
    (up1d, down1d), own = lax.optimization_barrier(((up1d, down1d), own))
    up2d, down2d = hop(up1d, 1, True), hop(down1d, -1, True)
    near = expert("td", where, weights, [(up1t, up1d), (down1t, down1d)], (3, 1), F32)
    far = expert("t", where, weights, [(up2t,), (down2t,)], (4, 0), BF16, near["hid"])
    far.update(expert("d", where, weights, [(up2d,), (down2d,)], (4, 0), BF16, far["f"]))

    def added(first, second):
        return (first + second.astype(F32)).astype(BF16)

    up_m, down_m = hop(far["m"][0], -1), hop(far["m"][1], 1)
    up_g, down_g = hop(far["g"][0], -1, True), hop(far["g"][1], 1, True)
    blocks = [
        (t0, d0, own["hid"][0], own["pair"][0]),
        (up1t, up1d, near["hid"][0], near["pair"][0]),
        (down1t, down1d, near["hid"][1], near["pair"][1]),
        (up2t, up2d, far["hid"][0], far["pair"][0]),
        (down2t, down2d, far["hid"][1], far["pair"][1]),
    ]
    sent = weight_grads(blocks, 1, BF16, (far["g"][0],))
    up_m, down_m = tied((up_m, down_m), sent)
    up_m1, down_m1 = added(near["m"][0], up_m), added(near["m"][1], down_m)
    sent = tied(sent, up_m1, down_m1)
    got = core_swap(sent)
    kept = weight_grads(blocks, 0, F32, (up_m1, down_m1))
    up_m1, down_m1 = hop(up_m1, -1, True), hop(down_m1, 1, True)
    up_g, down_g = tied((up_g, down_g), kept, got)
    up_g1, down_g1 = added(near["g"][0], up_g), added(near["g"][1], down_g)

    def side(value, half):
        return lax.dynamic_slice_in_dim(value, half * 2 * width, 2 * width, 1)

    here, there = owner // 2, 1 - owner // 2
    up_gb, down_gb = hop(side(up_g1, there), -1), hop(side(down_g1, there), 1)
    up_ga, down_ga = hop(side(up_g1, here), -1), hop(side(down_g1, here), 1)

    grads = kept + got.astype(F32)
    grad_in = grads[: 4 * width].reshape(1, 4 * width, 2, units)
    grad_out = jnp.concatenate(
        [grads[4 * width : 4 * width + units], grads[4 * width + units :]], axis=1
    )[None]
    (up_m1, down_m1), (grad_in, grad_out) = lax.optimization_barrier(((up_m1, down_m1), (grad_in, grad_out)))

    def rounded(value):
        value = value.astype(BF16)
        quarter = [lax.dynamic_slice_in_dim(value, c * width, width, 1) for c in (core, 1 - core)]
        quarter[1] = core_swap(quarter[1])
        return jnp.where(
            core == 0, jnp.concatenate(quarter, 0), jnp.concatenate([quarter[1], quarter[0]], 0)
        )

    total_m = own["m"][0] + up_m1.astype(F32) + down_m1.astype(F32)
    pair_m = pair_swap(side(total_m, there).astype(BF16))
    up_gb, down_gb = tied((up_gb, down_gb), total_m)
    pair_g = pair_swap((side(own["g"][0], there) + up_gb.astype(F32) + down_gb.astype(F32)).astype(BF16))
    mixed = rounded(side(total_m, here) + pair_m.astype(F32))
    up_ga, down_ga, pair_g = tied((up_ga, down_ga, pair_g), mixed)
    total_g = side(own["g"][0], here) + up_ga.astype(F32) + down_ga.astype(F32)
    token_grad = rounded(total_g + pair_g.astype(F32))
    return (mixed, token_grad, grad_in, grad_out)


def solution(mesh):
    placed = (
        P("dp", "owner"),
        P("dp", None),
        P("dp", None),
        P("dp", None, None, "owner"),
        P("dp", "owner", None),
        P("dp", "owner"),
    )
    return jax.shard_map(
        local,
        mesh=mesh,
        in_specs=placed,
        out_specs=(
            P("dp", "owner"),
            P("dp", "owner"),
            P("dp", None, None, "owner"),
            P("dp", "owner", None),
        ),
        check_vma=False,
    )
```

```python
import functools

import jax
import jax.numpy as jnp
from jax import lax
from jax.experimental import pallas as pl
from jax.experimental.pallas import tpu as pltpu
from jax.sharding import PartitionSpec as P

F32 = jnp.float32
BF16 = jnp.bfloat16
SLOTS = 8
PLANE = 16
NT = (((1,), (1,)), ((), ()))
TN = (((0,), (0,)), ((), ()))


def dot(lhs, rhs, dims=(((1,), (0,)), ((), ()))):
    return lax.dot_general(lhs, rhs, dims, preferred_element_type=F32)


def core_swap(value):
    return lax.ppermute(value, "owner", [(0, 1), (1, 0), (2, 3), (3, 2)])


def pair_swap(value):
    return lax.ppermute(value, "owner", [(0, 2), (1, 3), (2, 0), (3, 1)])


def hop(value, by, cross=False):
    perm = []
    for e in range(32):
        to = (e + by) % 32
        flip = 2 if cross and to // PLANE != e // PLANE else 0
        for o in range(4):
            perm.append((e * 4 + o, to * 4 + (o ^ flip)))
    return lax.ppermute(value, ("dp", "owner"), perm)


ANY = pl.BlockSpec(memory_space=pl.ANY)
HBM = pl.BlockSpec(memory_space=pltpu.HBM)
VMEM = pl.BlockSpec(memory_space=pltpu.VMEM)
SMEM = pl.BlockSpec(memory_space=pltpu.SMEM)
EXPERT_VMEM = 28 * 2**20
OTHER_VMEM = 60 * 2**20
SMALL_VMEM = 12 * 2**20


class Copies:
    def __init__(self, sems):
        self.sems, self.used = sems, 0

    def start(self, *pairs):
        copies = []
        for src, dst in pairs:
            copies.append(pltpu.make_async_copy(src, dst, self.sems.at[self.used]))
            self.used += 1
        for copy in copies:
            copy.start()
        return copies


def wait(copies):
    for copy in copies:
        copy.wait()


def pick_kernel(where, tokens, d_out, mine, rest, sems):
    rows, width = mine.shape[0], tokens.shape[1]
    copies, pairs = Copies(sems), []
    for core, out in ((where[1], mine), (1 - where[1], rest)):
        at = pl.ds(pl.multiple_of(core * rows, rows), rows)
        pairs.append((tokens.at[at, :], out.at[:, pl.ds(0, width)]))
        pairs.append((d_out.at[at, :], out.at[:, pl.ds(width, width)]))
    wait(copies.start(*pairs))


def join_kernel(where, mine, other, far_mine, far_other, extra, whole_t, whole_d, sems):
    width = mine.shape[1] // 2
    half, core = where[0], where[1]
    copies, pairs = Copies(sems), []
    for piece, h, c in (
        (mine, half, core),
        (other, half, 1 - core),
        (far_mine, 1 - half, core),
        (far_other, 1 - half, 1 - core),
    ):
        at = pl.ds(pl.multiple_of((h * 2 + c) * width, width), width)
        pairs.append((piece.at[:, pl.ds(0, width)], whole_t.at[:, at]))
        pairs.append((piece.at[:, pl.ds(width, width)], whole_d.at[:, at]))
    pairs.append((extra, whole_t.at[:, pl.ds(4 * width, extra.shape[1])]))
    wait(copies.start(*pairs))


def small_call(kernel, where, *operands, shapes):
    return pl.pallas_call(
        kernel,
        out_shape=tuple(jax.ShapeDtypeStruct(shape, BF16) for shape in shapes),
        in_specs=[SMEM] + [ANY] * len(operands),
        out_specs=(VMEM,) * len(shapes),
        scratch_shapes=[pltpu.SemaphoreType.DMA((9,))],
        compiler_params=pltpu.CompilerParams(vmem_limit_bytes=SMALL_VMEM),
        cost_estimate=pl.CostEstimate(flops=0, bytes_accessed=2 * 2**20, transcendentals=0),
    )(where, *operands)


def expert_kernel(phase, slots, n_in, where, *refs):
    ins, rest = refs[:n_in], list(refs[n_in:])
    with_t, with_d = phase != "d", phase != "t"
    count = len(slots)
    per = with_t + with_d
    sides = [ins[2 + per * i : 2 + per * (i + 1)] for i in range(count)]
    wide = 2 * ins[0].shape[1]
    units = (ins[0].shape[0] - wide) // 2
    halves = (slice(0, wide // 2), slice(wide // 2, wide))
    win = [w[:wide, :] for w in ins[:2]]
    wout = [[w[wide + k * units : wide + (k + 1) * units, :] for k in range(2)] for w in ins[:2]]
    rows = sides[0][0].shape[0]
    spans = [pl.ds(i * rows, rows) for i in range(count)]

    def take(n):
        return [rest.pop(0) for _ in range(n)]

    if with_t:
        mixed_outs, hid_outs = take(count), take(count)
    if phase == "t":
        fa_out, fb_out = take(2)
    if with_d:
        grad_outs, pair_outs = take(count), take(count)
    sems = rest.pop(-1)
    copies = Copies(sems)
    fa, fb = take(2)
    load_t, load_d, stores = [], [], []
    if with_t:
        xt, mixed, hid = take(3)
        for side, span in zip(sides, spans):
            load_t += copies.start((side[0], xt.at[span, :]))
    if with_d:
        xd, grad, pair = take(3)
        for side, span in zip(sides, spans):
            load_d += copies.start((side[-1], xd.at[span, :]))
    if not with_t:
        load_d += copies.start((ins[2 + per * count], fa), (ins[3 + per * count], fb))
    if with_t:
        wait(load_t)
        extra = xt[:, wide:].astype(F32)
        lane = lax.broadcasted_iota(jnp.int32, extra.shape, 1)
        row = lax.broadcasted_iota(jnp.int32, extra.shape, 0)
        slot = slots[0] if count == 1 else jnp.where(row < rows, slots[0], slots[1])
        mine = (lane == slot) | (lane == slot + SLOTS)
        share = jnp.sum(jnp.where(mine, extra, 0.0), axis=1, keepdims=True)
        for q in range(2):
            cols = slice(q * units, (q + 1) * units)
            gate_up = dot(xt[:, :wide], win[q])
            gate, up = gate_up[:, :units], gate_up[:, units:] + 1.0
            sig = jax.nn.sigmoid(1.702 * gate)
            gs = gate * sig
            sup = share * up
            hid[:, cols] = (sup * gs).astype(BF16)
            fa[:, cols] = sup * (sig + 1.702 * gs * (1.0 - sig))
            fb[:, cols] = share * gs
        for out, span in zip(hid_outs, spans):
            stores += copies.start((hid.at[span, :], out))
        if phase == "t":
            stores += copies.start((fa, fa_out), (fb, fb_out))
        for k, cols in enumerate(halves):
            total = dot(hid[:, :units], wout[0][k]) + dot(hid[:, units:], wout[1][k])
            mixed[:, cols] = total.astype(mixed.dtype)
        for out, span in zip(mixed_outs, spans):
            stores += copies.start((mixed.at[span, :], out))
    if with_d:
        wait(load_d)
        for q in range(2):
            cols = slice(q * units, (q + 1) * units)
            act = dot(xd[:, halves[0]], wout[q][0], NT) + dot(xd[:, halves[1]], wout[q][1], NT)
            pair[:, 2 * q * units : (2 * q + 1) * units] = (act * fa[:, cols]).astype(BF16)
            pair[:, (2 * q + 1) * units : (2 * q + 2) * units] = (act * fb[:, cols]).astype(BF16)
        for out, span in zip(pair_outs, spans):
            stores += copies.start((pair.at[span, :], out))
        grad[...] = (
            dot(pair[:, : 2 * units], win[0], NT) + dot(pair[:, 2 * units :], win[1], NT)
        ).astype(grad.dtype)
        for out, span in zip(grad_outs, spans):
            stores += copies.start((grad.at[span, :], out))
    wait(stores)


def expert(phase, where, weights, sides, slots, out_dtype, after=()):
    count = len(slots)
    rows = sides[0][0].shape[0]
    deep = count * rows
    wide = 2 * weights[0].shape[1]
    units = (weights[0].shape[0] - wide) // 2
    with_t, with_d = phase != "d", phase != "t"
    outs = []
    if with_t:
        outs += [((rows, wide), out_dtype)] * count + [((rows, 2 * units), BF16)] * count
    if phase == "t":
        outs += [((deep, 2 * units), F32)] * 2
    if with_d:
        outs += [((rows, wide), out_dtype)] * count + [((rows, 4 * units), BF16)] * count
    scratch = [((deep, 2 * units), F32)] * 2
    if with_t:
        scratch += [((deep, sides[0][0].shape[1]), BF16), ((deep, wide), out_dtype), ((deep, 2 * units), BF16)]
    if with_d:
        scratch += [((deep, wide), BF16), ((deep, wide), out_dtype), ((deep, 4 * units), BF16)]
    operands = (*weights, *[piece for side in sides for piece in side], *after)
    results = pl.pallas_call(
        functools.partial(expert_kernel, phase, slots, len(operands)),
        out_shape=tuple(jax.ShapeDtypeStruct(*o) for o in outs),
        in_specs=[SMEM] + [VMEM] * 2 + [HBM] * (len(operands) - 2),
        out_specs=(HBM,) * len(outs),
        scratch_shapes=[pltpu.VMEM(*v) for v in scratch] + [pltpu.SemaphoreType.DMA((16,))],
        compiler_params=pltpu.CompilerParams(vmem_limit_bytes=EXPERT_VMEM),
        cost_estimate=pl.CostEstimate(
            flops=2 * deep * wide * units * 2 * 3 * (with_t + with_d),
            bytes_accessed=12 * 2**20,
            transcendentals=deep * units * 2,
        ),
    )(where, *operands)
    results, named = list(results), {}
    for name, there, n in (
        ("m", with_t, count),
        ("hid", with_t, count),
        ("f", phase == "t", 2),
        ("g", with_d, count),
        ("pair", with_d, count),
    ):
        if there:
            named[name] = [results.pop(0) for _ in range(n)]
    return named


def weight_kernel(quarter, count, n_in, *refs):
    blocks = [refs[4 * j : 4 * j + 4] for j in range(count)]
    out, xt, xd, hid, pair, grads, sems = refs[n_in:]
    rows, wide = pair.shape[0] // count, xt.shape[1]
    units = hid.shape[1]
    copies = Copies(sems)
    first, second = [], []
    for j, (t, d, hids, pairs) in enumerate(blocks):
        block = pl.ds(j * rows, rows)
        first.append((pairs.at[:, pl.ds(2 * quarter * units, 2 * units)], pair.at[block, :]))
        first.append((t.at[:, pl.ds(0, wide)], xt.at[block, :]))
        second.append((hids.at[:, pl.ds(quarter * units, units)], hid.at[block, :]))
        second.append((d, xd.at[block, :]))
    first, second = copies.start(*first), copies.start(*second)
    wait(first)
    stores = []
    step = 256
    def keep(at, value):
        grads[at, :] = value.astype(grads.dtype)
        stores.extend(copies.start((grads.at[at, :], out.at[at, :])))

    for r in range(0, wide, step):
        keep(pl.ds(r, step), dot(xt[:, r : r + step], pair[...], TN))
    wait(second)
    for k in range(2):
        band = slice(k * wide // 2, (k + 1) * wide // 2)
        keep(pl.ds(wide + k * units, units), dot(hid[...], xd[:, band], TN))
    wait(stores)


def weight_grads(blocks, quarter, out_dtype, after=()):
    count = len(blocks)
    rows, wide = blocks[0][1].shape
    units = blocks[0][2].shape[1] // 2
    operands = [ref for block in blocks for ref in block] + list(after)
    depth = count * rows
    return pl.pallas_call(
        functools.partial(weight_kernel, quarter, count, len(operands)),
        out_shape=jax.ShapeDtypeStruct((wide + 2 * units, 2 * units), out_dtype),
        in_specs=[HBM] * len(operands),
        out_specs=HBM,
        scratch_shapes=[pltpu.VMEM((depth, n), BF16) for n in (wide, wide, units, 2 * units)]
        + [
            pltpu.VMEM((wide + 2 * units, 2 * units), out_dtype),
            pltpu.SemaphoreType.DMA((4 * count + 8,)),
        ],
        compiler_params=pltpu.CompilerParams(vmem_limit_bytes=OTHER_VMEM),
        cost_estimate=pl.CostEstimate(
            flops=2 * depth * wide * units * 3, bytes_accessed=18 * 2**20, transcendentals=0
        ),
    )(*operands)


def tied(values, *others):
    return lax.optimization_barrier((values, others))[0]


def local(tokens, routes, route_weights, w_in, w_out, d_out):
    position = lax.axis_index("dp")
    owner = lax.axis_index("owner")
    core = owner % 2
    where = jnp.stack([owner // 2, core]).astype(jnp.int32)
    rows = tokens.shape[0] // 2
    width = tokens.shape[1]
    units = w_out.shape[1]

    def part(value, index):
        return lax.dynamic_slice_in_dim(value, index * rows, rows, 0)

    ids = (position + jnp.arange(5, dtype=jnp.int32) - 2) % 32
    chosen = part(routes, core)[:, :, None] == ids[None, None, :]
    share = jnp.sum(jnp.where(chosen, part(route_weights, core)[:, :, None], 0.0), axis=1)
    high = lax.reduce_precision(share, 8, 7)
    low = share - high
    pad = ((0, 0), (0, SLOTS - 5))
    extra = jnp.concatenate([jnp.pad(high, pad), jnp.pad(low, pad)], axis=1)
    extra = jnp.pad(extra, ((0, 0), (0, 128 - 2 * SLOTS))).astype(BF16)
    mine, rest = small_call(pick_kernel, where, tokens, d_out, shapes=[(rows, 2 * width)] * 2)
    far_mine = pair_swap(mine)
    other = core_swap(rest)
    far_other = pair_swap(other)
    t0, d0 = small_call(
        join_kernel, where, mine, other, far_mine, far_other, extra,
        shapes=[(rows, 4 * width + 128), (rows, 4 * width)],
    )

    w_in, w_out = tied((w_in[0], w_out[0]), t0)
    packed = jnp.concatenate(
        [w_in.reshape(4 * width, 2 * units), w_out[:, : 2 * width], w_out[:, 2 * width :]], axis=0
    )
    weights = (packed, core_swap(packed))

    up1t, down1t = hop(t0, 1), hop(t0, -1)
    up1d, down1d = hop(d0, 1, True), hop(d0, -1, True)
    up2t, down2t = hop(up1t, 1), hop(down1t, -1)
    own = expert("td", where, weights, [(t0, d0)], (2,), F32)
    (up1d, down1d), own = lax.optimization_barrier(((up1d, down1d), own))
    up2d, down2d = hop(up1d, 1, True), hop(down1d, -1, True)
    near = expert("td", where, weights, [(up1t, up1d), (down1t, down1d)], (3, 1), F32)
    far = expert("t", where, weights, [(up2t,), (down2t,)], (4, 0), BF16, near["hid"])
    far.update(expert("d", where, weights, [(up2d,), (down2d,)], (4, 0), BF16, far["f"]))

    def added(first, second):
        return (first + second.astype(F32)).astype(BF16)

    up_m, down_m = hop(far["m"][0], -1), hop(far["m"][1], 1)
    up_g, down_g = hop(far["g"][0], -1, True), hop(far["g"][1], 1, True)
    blocks = [
        (t0, d0, own["hid"][0], own["pair"][0]),
        (up1t, up1d, near["hid"][0], near["pair"][0]),
        (down1t, down1d, near["hid"][1], near["pair"][1]),
        (up2t, up2d, far["hid"][0], far["pair"][0]),
        (down2t, down2d, far["hid"][1], far["pair"][1]),
    ]
    sent = weight_grads(blocks, 1, BF16, (far["g"][0],))
    up_m, down_m = tied((up_m, down_m), sent)
    up_m1, down_m1 = added(near["m"][0], up_m), added(near["m"][1], down_m)
    sent = tied(sent, up_m1, down_m1)
    got = core_swap(sent)
    kept = weight_grads(blocks, 0, F32, (up_m1, down_m1))
    up_m1, down_m1 = hop(up_m1, -1, True), hop(down_m1, 1, True)
    up_g, down_g = tied((up_g, down_g), kept, got)
    up_g1, down_g1 = added(near["g"][0], up_g), added(near["g"][1], down_g)

    def side(value, half):
        return lax.dynamic_slice_in_dim(value, half * 2 * width, 2 * width, 1)

    here, there = owner // 2, 1 - owner // 2
    up_gb, down_gb = hop(side(up_g1, there), -1), hop(side(down_g1, there), 1)
    up_ga, down_ga = hop(side(up_g1, here), -1), hop(side(down_g1, here), 1)

    grads = kept + got.astype(F32)
    grad_in = grads[: 4 * width].reshape(1, 4 * width, 2, units)
    grad_out = jnp.concatenate(
        [grads[4 * width : 4 * width + units], grads[4 * width + units :]], axis=1
    )[None]

    def rounded(value):
        value = value.astype(BF16)
        quarter = [lax.dynamic_slice_in_dim(value, c * width, width, 1) for c in (core, 1 - core)]
        quarter[1] = core_swap(quarter[1])
        return jnp.where(
            core == 0, jnp.concatenate(quarter, 0), jnp.concatenate([quarter[1], quarter[0]], 0)
        )

    total_m = own["m"][0] + up_m1.astype(F32) + down_m1.astype(F32)
    pair_m = pair_swap(side(total_m, there).astype(BF16))
    (up_gb, down_gb), (grad_in, grad_out) = lax.optimization_barrier((tied((up_gb, down_gb), total_m), (grad_in, grad_out)))
    pair_g = pair_swap((side(own["g"][0], there) + up_gb.astype(F32) + down_gb.astype(F32)).astype(BF16))
    mixed = rounded(side(total_m, here) + pair_m.astype(F32))
    up_ga, down_ga, pair_g = tied((up_ga, down_ga, pair_g), mixed)
    total_g = side(own["g"][0], here) + up_ga.astype(F32) + down_ga.astype(F32)
    token_grad = rounded(total_g + pair_g.astype(F32))
    return (mixed, token_grad, grad_in, grad_out)


def solution(mesh):
    placed = (
        P("dp", "owner"),
        P("dp", None),
        P("dp", None),
        P("dp", None, None, "owner"),
        P("dp", "owner", None),
        P("dp", "owner"),
    )
    return jax.shard_map(
        local,
        mesh=mesh,
        in_specs=placed,
        out_specs=(
            P("dp", "owner"),
            P("dp", "owner"),
            P("dp", None, None, "owner"),
            P("dp", "owner", None),
        ),
        check_vma=False,
    )
```
